32 devices in a mesh: groups: 2 (over x), wide: 8 (over z, y), narrow: 2 (over core).
Axes of the slice: x: 2, y: 2, z: 4, core: 2. Of those that a mesh axis runs over, the one named last changes fastest.
Arguments:
- activations: bfloat16 [1024, 9216], P('groups', ('narrow', 'wide')), parts along dimension 0, may hold values from -6 to 6
- up_weight: bfloat16 [9216, 9216], P('narrow', 'wide'), may hold values from -0.0625 to 0.0625
Outputs:
- hidden_out: bfloat16 [1024, 9216], P('groups', ('wide', 'narrow')), parts along dimension 0
The draws below stay inside these ranges and needn't reach their ends.
There are 2 independent parts, one for each index of `groups`. The reference program is written for one: setup_inputs(seed, part) draws one part's arguments, and reference() takes and returns one part's arrays. A program takes and returns all parts, laid end to end along the dimension named above; an argument that names none is the same for every part. Nothing has to cross between parts.
All inputs are finite; a program needn't handle non-finite values.
Results may differ from the reference program's by a relative error of at most 0.001.
Values may be sent and summed in bfloat16 or wider, within the bound.
A program may use at most 64 MiB of HBM per device.

```python
import jax
import jax.numpy as jnp

D = 9216
BATCH = 512
FF = 9216


def block_scale(rng, extent, shards, smallest, top_value):
    gain = 1.0
    for axis_at, blocks in shards:
        draws = jax.random.uniform(jax.random.fold_in(jax.random.fold_in(rng, 6), axis_at), (blocks,), jnp.float32, smallest / len(shards), top_value / len(shards))
        gain = gain * jnp.repeat(jnp.exp(draws), extent[axis_at] // blocks).reshape((-1,) + (1,) * (len(extent) - 1 - axis_at))
    return gain


def scatter_about(own_key, dims, width, reach, cuts=(), held_as=jnp.bfloat16):
    drawn = width * jax.random.normal(own_key, dims, jnp.float32)
    if cuts:
        drawn = drawn * block_scale(own_key, dims, cuts, -0.22, 0.18)
    return jnp.clip(drawn, -reach, reach).astype(held_as)


def setup_inputs(seed: int = 0, part: int = 0) -> dict:
    arg_keys = jax.random.split(jax.random.key(seed), 3)
    own_keys = jax.random.split(jax.random.fold_in(arg_keys[2], part), 3)
    return {
        "activations": scatter_about(own_keys[0], (BATCH, D), 1.0, 6.0, ((1, 16),)),
        "up_weight": scatter_about(arg_keys[1], (D, FF), D ** -0.5, 0.0625, ((0, 2), (1, 8))),
    }


def reference(activations, up_weight):
    pre_act = jnp.dot(activations, up_weight, preferred_element_type=jnp.float32)
    return jax.nn.gelu(pre_act, approximate=False).astype(jnp.bfloat16)
```

```python
import functools

import jax
import jax.numpy as jnp
from jax import lax
from jax.experimental import pallas as pl
from jax.experimental.pallas import tpu as pltpu
from jax.sharding import PartitionSpec as P

MESH = pl.DeviceIdType.MESH
Y = 2
CHUNKS = 4
LANES = 128
UP, DOWN, ACROSS = 0, 1, 2


def plain(activations, up_weight):
    half_features = lax.all_gather(activations, "wide", axis=1, tiled=True)
    partial_value = jnp.dot(half_features, up_weight, preferred_element_type=jnp.float32)
    own_sums = lax.psum_scatter(partial_value, "narrow", scatter_dimension=1, tiled=True)
    return jax.nn.gelu(own_sums, approximate=False).astype(jnp.bfloat16)


def kernel(
    n_wide, x_ref, w_ref, out_ref,
    buf, wv, w_rem, acc, other,
    w_sem, send_a, send_b, recv_a, recv_b, swap_send, swap_recv,
):
    rows_total, cols = x_ref.shape
    Z = n_wide // Y
    rows = rows_total // CHUNKS
    half = rows // 2
    main = cols // LANES * LANES
    rem = cols - main
    width = 2 * cols
    keep = other.shape[2]

    group = lax.axis_index("groups")
    me = lax.axis_index("wide")
    core = lax.axis_index("narrow")
    z, y = me // Y, me % Y

    def at(zz, yy):
        return zz * Y + yy

    targets = {
        UP: (group, me + Y, core),
        DOWN: (group, me - Y, core),
        ACROSS: (group, at(z, 1 - y), core),
    }
    partner = (group, me, 1 - core)

    w_copy = pltpu.make_async_copy(w_ref, wv, w_sem)
    w_copy.start()

    barrier = pltpu.get_barrier_semaphore()
    for peer in (targets[ACROSS], partner):
        pl.semaphore_signal(barrier, inc=1, device_id=peer, device_id_type=MESH)

    @pl.when(z < Z - 1)
    def _():
        pl.semaphore_signal(barrier, inc=1, device_id=targets[UP], device_id_type=MESH)

    @pl.when(z > 0)
    def _():
        pl.semaphore_signal(barrier, inc=1, device_id=targets[DOWN], device_id_type=MESH)

    for c in range(CHUNKS):
        top = x_ref[c * rows : c * rows + half, :]
        low = x_ref[c * rows + half : (c + 1) * rows, :]
        at_rows = pl.ds(c * half, half)
        buf[me, at_rows, 0:main] = top[:, :main]
        buf[me, at_rows, main : 2 * main] = low[:, :main]
        buf[me, at_rows, 2 * main : width] = jnp.concatenate([top[:, main:], low[:, main:]], axis=1)

    pl.semaphore_wait(barrier, 2 + (z < Z - 1).astype(jnp.int32) + (z > 0).astype(jnp.int32))

    def split(c):
        return width - LANES * (1 + c % 2)

    def copy(kind, c, src, way):
        at_rows = pl.ds(c * half, half)
        if kind == "a":
            ref = buf.at[src, at_rows, 0 : split(c)]
            sends, recvs = send_a, recv_a
        else:
            ref = buf.at[src, at_rows, split(c) : width]
            sends, recvs = send_b, recv_b
        return pltpu.make_async_remote_copy(
            src_ref=ref,
            dst_ref=ref,
            send_sem=sends.at[c, way, src],
            recv_sem=recvs.at[c, src],
            device_id=targets[way],
            device_id_type=MESH,
        )

    def along(kind, c, src, way):
        @pl.when((z < Z - 1) if way == UP else (z > 0))
        def _():
            copy(kind, c, src, way).start()

    def send_own(c):
        along("a", c, me, UP)
        along("a", c, me, DOWN)
        copy("b", c, me, ACROSS).start()
        copy("a", c, me, ACROSS).start()
        along("b", c, me, UP)
        along("b", c, me, DOWN)

    def arrivals(c, d):
        for way, zs in ((UP, z - d), (DOWN, z + d)):
            @pl.when((zs >= 0) & (zs < Z))
            def _():
                src = at(zs, y)
                copy("a", c, src, way).wait_recv()
                along("a", c, src, way)
                copy("a", c, src, ACROSS).start()

        if d == 1:
            src = at(z, 1 - y)
            copy("b", c, src, ACROSS).wait_recv()
            along("b", c, src, UP)
            along("b", c, src, DOWN)
        for way, zs in ((UP, z - d), (DOWN, z + d)):
            @pl.when((zs >= 0) & (zs < Z))
            def _():
                for yy in range(Y):
                    src = at(zs, yy)
                    copy("b", c, src, way).wait_recv()
                    along("b", c, src, way)

    def wait_across(c):
        for zs in range(Z):
            copy("a", c, at(zs, 1 - y), ACROSS).wait_recv()

    def dot(a, b):
        return jnp.dot(a, b, preferred_element_type=jnp.float32)

    def remainders(c):
        at_rows = pl.ds(c * half, half)
        pieces = [buf[w, at_rows, 2 * main : width] for w in range(n_wide)]
        top = jnp.concatenate([p[:, :rem] for p in pieces], axis=1)
        low = jnp.concatenate([p[:, rem:] for p in pieces], axis=1)
        acc[c] = dot(jnp.concatenate([top, low], axis=0), w_rem[...])

    def mains(c, first, last):
        at_rows = pl.ds(c * half, half)

        def step(w, carry):
            lhs = jnp.concatenate(
                [buf[w, at_rows, 0:main], buf[w, at_rows, main : 2 * main]], axis=0
            )
            acc[c] += dot(lhs, wv[pl.ds(pl.multiple_of(w * cols, 64), main), :])
            return carry

        lax.fori_loop(first, last, step, 0)

    def swap(c):
        start = pl.multiple_of((1 - core) * (acc.shape[2] - keep), LANES)
        return pltpu.make_async_remote_copy(
            src_ref=acc.at[c, :, pl.ds(start, keep)],
            dst_ref=other.at[c],
            send_sem=swap_send.at[c],
            recv_sem=swap_recv.at[c],
            device_id=partner,
            device_id_type=MESH,
        )

    def finish(c):
        swap(c).wait_recv()
        start = pl.multiple_of(core * (acc.shape[2] - keep), LANES)
        v = acc[c, :, pl.ds(start, keep)] + other[c]
        hidden = v * (1.0 + lax.erf(v * 0.7071067811865476)) * 0.5
        n = out_ref.shape[1]
        mine = jnp.where(core == 0, hidden[:, :n], hidden[:, keep - n :])
        out_ref[c * rows : (c + 1) * rows, :] = mine.astype(out_ref.dtype)

    send_own(0)
    send_own(1)
    w_copy.wait()
    for w in range(n_wide):
        w_rem[w * rem : (w + 1) * rem, :] = wv[w * cols + main : (w + 1) * cols, :]

    parts = [(0, 3), (3, 6), (6, n_wide)]
    for c in range(CHUNKS):
        if 1 <= c < CHUNKS - 1:
            send_own(c + 1)
        for d in range(1, Z):
            arrivals(c, d)
            if c > 0:
                if d == 1:
                    wait_across(c - 1)
                    remainders(c - 1)
                mains(c - 1, *parts[d - 1])
        if c > 0:
            swap(c - 1).start()
        if c > 1:
            finish(c - 2)
    last = CHUNKS - 1
    wait_across(last)
    remainders(last)
    mains(last, 0, n_wide)
    swap(last).start()
    finish(last - 1)
    finish(last)

    for c in range(CHUNKS):
        swap(c).wait_send()
        copy("b", c, me, ACROSS).wait_send()
        for zs in range(Z):
            copy("a", c, at(zs, y), ACROSS).wait_send()

            @pl.when((zs <= z) & (z < Z - 1))
            def _():
                copy("a", c, at(zs, y), UP).wait_send()
                for yy in range(Y):
                    copy("b", c, at(zs, yy), UP).wait_send()

            @pl.when((zs >= z) & (z > 0))
            def _():
                copy("a", c, at(zs, y), DOWN).wait_send()
                for yy in range(Y):
                    copy("b", c, at(zs, yy), DOWN).wait_send()


def fused(n_wide, activations, up_weight):
    rows, cols = activations.shape
    depth, units = up_weight.shape
    rem = cols % LANES
    keep = (units // 2 + LANES - 1) // LANES * LANES
    return pl.pallas_call(
        functools.partial(kernel, n_wide),
        out_shape=jax.ShapeDtypeStruct((rows, units // 2), jnp.bfloat16),
        in_specs=[
            pl.BlockSpec(memory_space=pltpu.VMEM),
            pl.BlockSpec(memory_space=pl.ANY),
        ],
        out_specs=pl.BlockSpec(memory_space=pltpu.VMEM),
        scratch_shapes=[
            pltpu.VMEM((n_wide, rows // 2, 2 * cols), jnp.bfloat16),
            pltpu.VMEM((depth, units), jnp.bfloat16),
            pltpu.VMEM((n_wide * rem, units), jnp.bfloat16),
            pltpu.VMEM((CHUNKS, rows // CHUNKS, units), jnp.float32),
            pltpu.VMEM((CHUNKS, rows // CHUNKS, keep), jnp.float32),
            pltpu.SemaphoreType.DMA,
            pltpu.SemaphoreType.DMA((CHUNKS, 3, n_wide)),
            pltpu.SemaphoreType.DMA((CHUNKS, 3, n_wide)),
            pltpu.SemaphoreType.DMA((CHUNKS, n_wide)),
            pltpu.SemaphoreType.DMA((CHUNKS, n_wide)),
            pltpu.SemaphoreType.DMA((CHUNKS,)),
            pltpu.SemaphoreType.DMA((CHUNKS,)),
        ],
        compiler_params=pltpu.CompilerParams(
            collective_id=0, has_side_effects=True, vmem_limit_bytes=48 * 2**20
        ),
        cost_estimate=pl.CostEstimate(
            flops=2 * rows * depth * units,
            bytes_accessed=2 * depth * units,
            transcendentals=rows * units // 2,
        ),
    )(activations, up_weight)


def solution(mesh):
    n_wide = mesh.shape["wide"]
    body = functools.partial(fused, n_wide) if n_wide == 4 * Y else plain
    return jax.shard_map(
        body,
        mesh=mesh,
        in_specs=(P("groups", ("narrow", "wide")), P("narrow", "wide")),
        out_specs=P("groups", ("wide", "narrow")),
        check_vma=False,
    )
```

```python
import functools

import jax
import jax.numpy as jnp
from jax import lax
from jax.experimental import pallas as pl
from jax.experimental.pallas import tpu as pltpu
from jax.sharding import PartitionSpec as P

MESH = pl.DeviceIdType.MESH
Y = 2
GROUPS = (64, 64, 48, 32, 48)
LANES = 128
UP, DOWN, ACROSS = 0, 1, 2


def plain(activations, up_weight):
    half_features = lax.all_gather(activations, "wide", axis=1, tiled=True)
    partial_value = jnp.dot(half_features, up_weight, preferred_element_type=jnp.float32)
    own_sums = lax.psum_scatter(partial_value, "narrow", scatter_dimension=1, tiled=True)
    return jax.nn.gelu(own_sums, approximate=False).astype(jnp.bfloat16)


def kernel(
    n_wide, x_ref, w_ref, out_ref,
    buf, wv, acc, other,
    w_sem, send_sem, recv_sem, swap_send, swap_recv,
):
    rows, cols = x_ref.shape
    Z = n_wide // Y
    pairs = rows // 2
    main = cols // LANES * LANES
    rem = cols - main
    width = 2 * cols
    units = wv.shape[1]
    keep = other.shape[2]
    n_a = len(GROUPS) - 1
    last = n_a
    offsets = [sum(GROUPS[:i]) for i in range(len(GROUPS) + 1)]

    group = lax.axis_index("groups")
    me = lax.axis_index("wide")
    core = lax.axis_index("narrow")
    z, y = me // Y, me % Y
    far = jnp.where(z < Z // 2, Z - 1, 0)

    def at(zz, yy):
        return zz * Y + yy

    targets = {
        UP: (group, me + Y, core),
        DOWN: (group, me - Y, core),
        ACROSS: (group, at(z, 1 - y), core),
    }
    partner = (group, me, 1 - core)

    w_copy = pltpu.make_async_copy(w_ref, wv, w_sem)
    w_copy.start()

    barrier = pltpu.get_barrier_semaphore()
    for peer in (targets[ACROSS], partner):
        pl.semaphore_signal(barrier, inc=1, device_id=peer, device_id_type=MESH)

    @pl.when(z < Z - 1)
    def _():
        pl.semaphore_signal(barrier, inc=1, device_id=targets[UP], device_id_type=MESH)

    @pl.when(z > 0)
    def _():
        pl.semaphore_signal(barrier, inc=1, device_id=targets[DOWN], device_id_type=MESH)

    top = x_ref[:pairs, :]
    low = x_ref[pairs:, :]
    buf[me, :, 0:main] = top[:, :main]
    buf[me, :, main : 2 * main] = low[:, :main]
    buf[me, :, 2 * main : width] = jnp.concatenate([top[:, main:], low[:, main:]], axis=1)

    pl.semaphore_wait(barrier, 2 + (z < Z - 1).astype(jnp.int32) + (z > 0).astype(jnp.int32))

    def copy(c, src, way):
        ref = buf.at[src, pl.ds(offsets[c], GROUPS[c]), :]
        return pltpu.make_async_remote_copy(
            src_ref=ref,
            dst_ref=ref,
            send_sem=send_sem.at[c, way, src],
            recv_sem=recv_sem.at[c, src],
            device_id=targets[way],
            device_id_type=MESH,
        )

    def along(c, src, way):
        @pl.when((z < Z - 1) if way == UP else (z > 0))
        def _():
            copy(c, src, way).start()

    def stops(d):
        return (UP, z - d), (DOWN, z + d)

    def pass_on(c, d):
        for way, zs in stops(d):
            @pl.when((zs >= 0) & (zs < Z))
            def _():
                for yy in range(Y) if c == last else (y,):
                    src = at(zs, yy)
                    copy(c, src, way).wait_recv()
                    along(c, src, way)
                    if c != last:
                        copy(c, src, ACROSS).start()

    def wait_across(zs):
        for c in range(n_a):
            copy(c, at(zs, 1 - y), ACROSS).wait_recv()

    def add(src, first, n, fresh=False):
        block = buf[src, pl.ds(first, n), :]
        left = jnp.concatenate([block[:, :main], block[:, 2 * main : 2 * main + rem]], axis=1)
        right = jnp.concatenate([block[:, main : 2 * main], block[:, 2 * main + rem :]], axis=1)
        value = jnp.dot(
            jnp.concatenate([left, right], axis=0),
            wv[pl.ds(pl.multiple_of(src * cols, 64), cols), :],
            preferred_element_type=jnp.float32,
        ).reshape(2, n, units)
        if fresh:
            acc[:, pl.ds(first, n), :] = value
        else:
            acc[:, pl.ds(first, n), :] += value

    def add_at(d, across):
        def step(i, carry):
            zs = z + d * (2 * i - 1)

            @pl.when((zs >= 0) & (zs < Z) & (zs != far))
            def _():
                if across:
                    wait_across(zs)
                add(at(zs, 1 - y if across else y), 0, pairs)

            return carry

        lax.fori_loop(0, 2, step, 0)

    def swap(c):
        start = pl.multiple_of((1 - core) * (units - keep), LANES)
        at_rows = pl.ds(offsets[c], GROUPS[c])
        return pltpu.make_async_remote_copy(
            src_ref=acc.at[:, at_rows, pl.ds(start, keep)],
            dst_ref=other.at[:, at_rows, :],
            send_sem=swap_send.at[c],
            recv_sem=swap_recv.at[c],
            device_id=partner,
            device_id_type=MESH,
        )

    def finish(c):
        swap(c).wait_recv()
        start = pl.multiple_of(core * (units - keep), LANES)
        at_rows = pl.ds(offsets[c], GROUPS[c])
        v = acc[:, at_rows, pl.ds(start, keep)] + other[:, at_rows, :]
        hidden = v * (1.0 + lax.erf(v * 0.7071067811865476)) * 0.5
        n = out_ref.shape[1]
        mine = jnp.where(core == 0, hidden[:, :, :n], hidden[:, :, keep - n :])
        mine = mine.astype(out_ref.dtype)
        for i in range(2):
            out_ref[pl.ds(i * pairs + offsets[c], GROUPS[c]), :] = mine[i]

    copy(last, me, ACROSS).start()
    for c in range(n_a):
        along(c, me, UP)
        along(c, me, DOWN)
        copy(c, me, ACROSS).start()
    along(last, me, UP)
    along(last, me, DOWN)
    copy(last, at(z, 1 - y), ACROSS).wait_recv()
    along(last, at(z, 1 - y), UP)
    along(last, at(z, 1 - y), DOWN)

    def start_sums():
        w_copy.wait()
        add(me, 0, pairs, fresh=True)

    def peer_sums():
        wait_across(z)
        add(at(z, 1 - y), 0, pairs)

    tasks = {
        (1, 0): start_sums,
        (2, 0): lambda: add_at(1, False),
        (2, 1): peer_sums,
        (3, 0): lambda: add_at(2, False),
        (3, 1): lambda: add_at(1, True),
    }
    for d in range(1, Z):
        for c in range(n_a):
            pass_on(c, d)
            if (d, c) in tasks:
                tasks[d, c]()
        if d < Z - 1:
            pass_on(last, d)

    add_at(2, True)
    add(at(far, y), 0, offsets[last])
    for c in range(n_a):
        copy(c, at(far, 1 - y), ACROSS).wait_recv()
        add(at(far, 1 - y), offsets[c], GROUPS[c])
        swap(c).start()
        if c > 0:
            finish(c - 1)
    pass_on(last, Z - 1)
    for yy in range(Y):
        add(at(far, yy), offsets[last], GROUPS[last])
    swap(last).start()
    finish(last - 1)
    finish(last)

    copy(last, me, ACROSS).wait_send()
    for c in range(len(GROUPS)):
        swap(c).wait_send()
        for zs in range(Z):
            if c != last:
                copy(c, at(zs, y), ACROSS).wait_send()
            for way, sent in ((UP, (zs <= z) & (z < Z - 1)), (DOWN, (zs >= z) & (z > 0))):
                @pl.when(sent)
                def _():
                    for yy in range(Y) if c == last else (y,):
                        copy(c, at(zs, yy), way).wait_send()


def fused(n_wide, activations, up_weight):
    rows, cols = activations.shape
    depth, units = up_weight.shape
    keep = (units // 2 + LANES - 1) // LANES * LANES
    return pl.pallas_call(
        functools.partial(kernel, n_wide),
        out_shape=jax.ShapeDtypeStruct((rows, units // 2), jnp.bfloat16),
        in_specs=[
            pl.BlockSpec(memory_space=pltpu.VMEM),
            pl.BlockSpec(memory_space=pl.ANY),
        ],
        out_specs=pl.BlockSpec(memory_space=pltpu.VMEM),
        scratch_shapes=[
            pltpu.VMEM((n_wide, rows // 2, 2 * cols), jnp.bfloat16),
            pltpu.VMEM((depth, units), jnp.bfloat16),
            pltpu.VMEM((2, rows // 2, units), jnp.float32),
            pltpu.VMEM((2, rows // 2, keep), jnp.float32),
            pltpu.SemaphoreType.DMA,
            pltpu.SemaphoreType.DMA((len(GROUPS), 3, n_wide)),
            pltpu.SemaphoreType.DMA((len(GROUPS), n_wide)),
            pltpu.SemaphoreType.DMA((len(GROUPS),)),
            pltpu.SemaphoreType.DMA((len(GROUPS),)),
        ],
        compiler_params=pltpu.CompilerParams(
            collective_id=0, has_side_effects=True, vmem_limit_bytes=48 * 2**20
        ),
        cost_estimate=pl.CostEstimate(
            flops=2 * rows * depth * units,
            bytes_accessed=2 * depth * units,
            transcendentals=rows * units // 2,
        ),
    )(activations, up_weight)


def solution(mesh):
    n_wide = mesh.shape["wide"]
    body = functools.partial(fused, n_wide) if n_wide == 4 * Y else plain
    return jax.shard_map(
        body,
        mesh=mesh,
        in_specs=(P("groups", ("narrow", "wide")), P("narrow", "wide")),
        out_specs=P("groups", ("wide", "narrow")),
        check_vma=False,
    )
```

```python
import functools

import jax
import jax.numpy as jnp
from jax import lax
from jax.experimental import pallas as pl
from jax.experimental.pallas import tpu as pltpu
from jax.sharding import PartitionSpec as P

MESH = pl.DeviceIdType.MESH
Y = 2
GROUPS = (64, 64, 64, 32, 32)
LANES = 128
UP, DOWN, ACROSS = 0, 1, 2


def plain(activations, up_weight):
    half_features = lax.all_gather(activations, "wide", axis=1, tiled=True)
    partial_value = jnp.dot(half_features, up_weight, preferred_element_type=jnp.float32)
    own_sums = lax.psum_scatter(partial_value, "narrow", scatter_dimension=1, tiled=True)
    return jax.nn.gelu(own_sums, approximate=False).astype(jnp.bfloat16)


def kernel(
    n_wide, x_ref, w_ref, out_ref,
    buf, wv, acc, other,
    w_sem, send_sem, recv_sem, swap_send, swap_recv,
):
    cols, rows = x_ref.shape
    Z = n_wide // Y
    pairs = rows // 2
    main = cols // LANES * LANES
    rem = cols - main
    width = 2 * cols
    units = wv.shape[1]
    keep = other.shape[2]
    n_a = len(GROUPS) - 1
    last = n_a
    offsets = [sum(GROUPS[:i]) for i in range(len(GROUPS) + 1)]

    group = lax.axis_index("groups")
    me = lax.axis_index("wide")
    core = lax.axis_index("narrow")
    z, y = me // Y, me % Y
    far = jnp.where(z < Z // 2, Z - 1, 0)

    def at(zz, yy):
        return zz * Y + yy

    targets = {
        UP: (group, me + Y, core),
        DOWN: (group, me - Y, core),
        ACROSS: (group, at(z, 1 - y), core),
    }
    partner = (group, me, 1 - core)

    w_copy = pltpu.make_async_copy(w_ref, wv, w_sem)
    w_copy.start()

    barrier = pltpu.get_barrier_semaphore()
    for peer in (targets[ACROSS], partner):
        pl.semaphore_signal(barrier, inc=1, device_id=peer, device_id_type=MESH)

    @pl.when(z < Z - 1)
    def _():
        pl.semaphore_signal(barrier, inc=1, device_id=targets[UP], device_id_type=MESH)

    @pl.when(z > 0)
    def _():
        pl.semaphore_signal(barrier, inc=1, device_id=targets[DOWN], device_id_type=MESH)

    own = x_ref[...].T
    top, low = own[:pairs], own[pairs:]
    buf[me, :, 0:main] = top[:, :main]
    buf[me, :, main : 2 * main] = low[:, :main]
    buf[me, :, 2 * main : width] = jnp.concatenate([top[:, main:], low[:, main:]], axis=1)

    pl.semaphore_wait(barrier, 2 + (z < Z - 1).astype(jnp.int32) + (z > 0).astype(jnp.int32))

    def copy(c, src, way):
        ref = buf.at[src, pl.ds(offsets[c], GROUPS[c]), :]
        return pltpu.make_async_remote_copy(
            src_ref=ref,
            dst_ref=ref,
            send_sem=send_sem.at[c, way, src],
            recv_sem=recv_sem.at[c, src],
            device_id=targets[way],
            device_id_type=MESH,
        )

    def along(c, src, way):
        @pl.when((z < Z - 1) if way == UP else (z > 0))
        def _():
            copy(c, src, way).start()

    def stops(d):
        return (UP, z - d), (DOWN, z + d)

    def pass_on(c, d):
        for way, zs in stops(d):
            @pl.when((zs >= 0) & (zs < Z))
            def _():
                for yy in range(Y) if c == last else (y,):
                    src = at(zs, yy)
                    copy(c, src, way).wait_recv()
                    along(c, src, way)
                    if c != last:
                        copy(c, src, ACROSS).start()

    def wait_across(zs):
        for c in range(n_a):
            copy(c, at(zs, 1 - y), ACROSS).wait_recv()

    def add(src, first, n, fresh=False):
        block = buf[src, pl.ds(first, n), :]
        left = jnp.concatenate([block[:, :main], block[:, 2 * main : 2 * main + rem]], axis=1)
        right = jnp.concatenate([block[:, main : 2 * main], block[:, 2 * main + rem :]], axis=1)
        value = jnp.dot(
            jnp.concatenate([left, right], axis=0),
            wv[pl.ds(pl.multiple_of(src * cols, 64), cols), :],
            preferred_element_type=jnp.float32,
        ).reshape(2, n, units)
        if fresh:
            acc[:, pl.ds(first, n), :] = value
        else:
            acc[:, pl.ds(first, n), :] += value

    def add_at(d, across):
        def step(i, carry):
            zs = z + d * (2 * i - 1)

            @pl.when((zs >= 0) & (zs < Z) & (zs != far))
            def _():
                if across:
                    wait_across(zs)
                add(at(zs, 1 - y if across else y), 0, pairs)

            return carry

        lax.fori_loop(0, 2, step, 0)

    def swap(c):
        start = pl.multiple_of((1 - core) * (units - keep), LANES)
        at_rows = pl.ds(offsets[c], GROUPS[c])
        return pltpu.make_async_remote_copy(
            src_ref=acc.at[:, at_rows, pl.ds(start, keep)],
            dst_ref=other.at[:, at_rows, :],
            send_sem=swap_send.at[c],
            recv_sem=swap_recv.at[c],
            device_id=partner,
            device_id_type=MESH,
        )

    def finish(c):
        swap(c).wait_recv()
        start = pl.multiple_of(core * (units - keep), LANES)
        at_rows = pl.ds(offsets[c], GROUPS[c])
        v = acc[:, at_rows, pl.ds(start, keep)] + other[:, at_rows, :]
        hidden = v * (1.0 + lax.erf(v * 0.7071067811865476)) * 0.5
        n = out_ref.shape[1]
        mine = jnp.where(core == 0, hidden[:, :, :n], hidden[:, :, keep - n :])
        mine = mine.astype(out_ref.dtype)
        for i in range(2):
            out_ref[pl.ds(i * pairs + offsets[c], GROUPS[c]), :] = mine[i]

    copy(last, me, ACROSS).start()
    for c in range(n_a):
        along(c, me, UP)
        along(c, me, DOWN)
        copy(c, me, ACROSS).start()
    along(last, me, UP)
    along(last, me, DOWN)
    copy(last, at(z, 1 - y), ACROSS).wait_recv()
    along(last, at(z, 1 - y), UP)
    along(last, at(z, 1 - y), DOWN)

    def start_sums():
        w_copy.wait()
        add(me, 0, pairs, fresh=True)

    def peer_sums():
        wait_across(z)
        add(at(z, 1 - y), 0, pairs)

    tasks = {
        (1, 0): start_sums,
        (2, 0): lambda: add_at(1, False),
        (2, 1): peer_sums,
        (3, 0): lambda: add_at(2, False),
        (3, 1): lambda: add_at(1, True),
    }
    for d in range(1, Z):
        for c in range(n_a):
            pass_on(c, d)
            if (d, c) in tasks:
                tasks[d, c]()
        if d < Z - 1:
            pass_on(last, d)

    add_at(2, True)
    add(at(far, y), 0, offsets[last])
    for c in range(n_a):
        copy(c, at(far, 1 - y), ACROSS).wait_recv()
        add(at(far, 1 - y), offsets[c], GROUPS[c])
        swap(c).start()
        if c > 0:
            finish(c - 1)
    pass_on(last, Z - 1)
    for yy in range(Y):
        add(at(far, yy), offsets[last], GROUPS[last])
    swap(last).start()
    finish(last - 1)
    finish(last)

    copy(last, me, ACROSS).wait_send()
    for c in range(len(GROUPS)):
        swap(c).wait_send()
        for zs in range(Z):
            if c != last:
                copy(c, at(zs, y), ACROSS).wait_send()
            for way, sent in ((UP, (zs <= z) & (z < Z - 1)), (DOWN, (zs >= z) & (z > 0))):
                @pl.when(sent)
                def _():
                    for yy in range(Y) if c == last else (y,):
                        copy(c, at(zs, yy), way).wait_send()


def fused(n_wide, activations, up_weight):
    rows, cols = activations.shape
    depth, units = up_weight.shape
    keep = (units // 2 + LANES - 1) // LANES * LANES
    return pl.pallas_call(
        functools.partial(kernel, n_wide),
        out_shape=jax.ShapeDtypeStruct((rows, units // 2), jnp.bfloat16),
        in_specs=[
            pl.BlockSpec(memory_space=pltpu.VMEM),
            pl.BlockSpec(memory_space=pl.ANY),
        ],
        out_specs=pl.BlockSpec(memory_space=pltpu.VMEM),
        scratch_shapes=[
            pltpu.VMEM((n_wide, rows // 2, 2 * cols), jnp.bfloat16),
            pltpu.VMEM((depth, units), jnp.bfloat16),
            pltpu.VMEM((2, rows // 2, units), jnp.float32),
            pltpu.VMEM((2, rows // 2, keep), jnp.float32),
            pltpu.SemaphoreType.DMA,
            pltpu.SemaphoreType.DMA((len(GROUPS), 3, n_wide)),
            pltpu.SemaphoreType.DMA((len(GROUPS), n_wide)),
            pltpu.SemaphoreType.DMA((len(GROUPS),)),
            pltpu.SemaphoreType.DMA((len(GROUPS),)),
        ],
        compiler_params=pltpu.CompilerParams(
            collective_id=0, has_side_effects=True, vmem_limit_bytes=48 * 2**20
        ),
        cost_estimate=pl.CostEstimate(
            flops=2 * rows * depth * units,
            bytes_accessed=2 * depth * units,
            transcendentals=rows * units // 2,
        ),
    )(activations.T, up_weight)


def solution(mesh):
    n_wide = mesh.shape["wide"]
    body = functools.partial(fused, n_wide) if n_wide == 4 * Y else plain
    return jax.shard_map(
        body,
        mesh=mesh,
        in_specs=(P("groups", ("narrow", "wide")), P("narrow", "wide")),
        out_specs=P("groups", ("wide", "narrow")),
        check_vma=False,
    )
```

```python
import functools

import jax
import jax.numpy as jnp
from jax import lax
from jax.experimental import pallas as pl
from jax.experimental.pallas import tpu as pltpu
from jax.sharding import PartitionSpec as P

MESH = pl.DeviceIdType.MESH
Y = 2
GROUPS = (64, 64, 64, 32, 32)
LANES = 128
UP, DOWN, ACROSS = 0, 1, 2


def plain(activations, up_weight):
    half_features = lax.all_gather(activations, "wide", axis=1, tiled=True)
    partial_value = jnp.dot(half_features, up_weight, preferred_element_type=jnp.float32)
    own_sums = lax.psum_scatter(partial_value, "narrow", scatter_dimension=1, tiled=True)
    return jax.nn.gelu(own_sums, approximate=False).astype(jnp.bfloat16)


def kernel(
    n_wide, x_ref, w_ref, out_ref,
    buf, wv, acc, other,
    w_sem, send_sem, recv_sem, swap_send, swap_recv,
):
    cols, rows = x_ref.shape
    Z = n_wide // Y
    pairs = rows // 2
    main = cols // LANES * LANES
    rem = cols - main
    width = 2 * cols
    units = wv.shape[1]
    keep = other.shape[2]
    n_a = len(GROUPS) - 1
    last = n_a
    offsets = [sum(GROUPS[:i]) for i in range(len(GROUPS) + 1)]

    group = lax.axis_index("groups")
    me = lax.axis_index("wide")
    core = lax.axis_index("narrow")
    z, y = me // Y, me % Y
    far = jnp.where(z < Z // 2, Z - 1, 0)

    def at(zz, yy):
        return zz * Y + yy

    targets = {
        UP: (group, me + Y, core),
        DOWN: (group, me - Y, core),
        ACROSS: (group, at(z, 1 - y), core),
    }
    partner = (group, me, 1 - core)

    w_copy = pltpu.make_async_copy(w_ref, wv, w_sem)
    w_copy.start()

    barrier = pltpu.get_barrier_semaphore()
    for peer in (targets[ACROSS], partner):
        pl.semaphore_signal(barrier, inc=1, device_id=peer, device_id_type=MESH)

    @pl.when(z < Z - 1)
    def _():
        pl.semaphore_signal(barrier, inc=1, device_id=targets[UP], device_id_type=MESH)

    @pl.when(z > 0)
    def _():
        pl.semaphore_signal(barrier, inc=1, device_id=targets[DOWN], device_id_type=MESH)

    own = x_ref[...].T
    top, low = own[:pairs], own[pairs:]
    buf[me, :, 0:main] = top[:, :main]
    buf[me, :, main : 2 * main] = low[:, :main]
    buf[me, :, 2 * main : width] = jnp.concatenate([top[:, main:], low[:, main:]], axis=1)

    pl.semaphore_wait(barrier, 2 + (z < Z - 1).astype(jnp.int32) + (z > 0).astype(jnp.int32))

    def copy(c, src, way):
        ref = buf.at[src, pl.ds(offsets[c], GROUPS[c]), :]
        return pltpu.make_async_remote_copy(
            src_ref=ref,
            dst_ref=ref,
            send_sem=send_sem.at[c, way, src],
            recv_sem=recv_sem.at[c, src],
            device_id=targets[way],
            device_id_type=MESH,
        )

    def along(c, src, way):
        @pl.when((z < Z - 1) if way == UP else (z > 0))
        def _():
            copy(c, src, way).start()

    def stops(d):
        return (UP, z - d), (DOWN, z + d)

    def pass_on(c, d):
        for way, zs in stops(d):
            @pl.when((zs >= 0) & (zs < Z))
            def _():
                for yy in range(Y) if c == last else (y,):
                    src = at(zs, yy)
                    copy(c, src, way).wait_recv()
                    along(c, src, way)
                    if c != last:
                        copy(c, src, ACROSS).start()

    def wait_across(zs):
        for c in range(n_a):
            copy(c, at(zs, 1 - y), ACROSS).wait_recv()

    def add(src, first, n, fresh=False):
        block = buf[src, pl.ds(first, n), :]
        left = jnp.concatenate([block[:, :main], block[:, 2 * main : 2 * main + rem]], axis=1)
        right = jnp.concatenate([block[:, main : 2 * main], block[:, 2 * main + rem :]], axis=1)
        value = jnp.dot(
            jnp.concatenate([left, right], axis=0),
            wv[pl.ds(pl.multiple_of(src * cols, 64), cols), :],
            preferred_element_type=jnp.float32,
        ).reshape(2, n, units)
        if fresh:
            acc[:, pl.ds(first, n), :] = value
        else:
            acc[:, pl.ds(first, n), :] += value

    def add_at(d, across):
        def step(i, carry):
            zs = z + d * (2 * i - 1)

            @pl.when((zs >= 0) & (zs < Z) & (zs != far))
            def _():
                if across:
                    wait_across(zs)
                add(at(zs, 1 - y if across else y), 0, pairs)

            return carry

        lax.fori_loop(0, 2, step, 0)

    def swap(c):
        start = pl.multiple_of((1 - core) * (units - keep), LANES)
        at_rows = pl.ds(offsets[c], GROUPS[c])
        return pltpu.make_async_remote_copy(
            src_ref=acc.at[:, at_rows, pl.ds(start, keep)],
            dst_ref=other.at[:, at_rows, :],
            send_sem=swap_send.at[c],
            recv_sem=swap_recv.at[c],
            device_id=partner,
            device_id_type=MESH,
        )

    def finish(c):
        swap(c).wait_recv()
        start = pl.multiple_of(core * (units - keep), LANES)
        at_rows = pl.ds(offsets[c], GROUPS[c])
        v = acc[:, at_rows, pl.ds(start, keep)] + other[:, at_rows, :]
        hidden = v * (1.0 + lax.erf(v * 0.7071067811865476)) * 0.5
        n = out_ref.shape[1]
        mine = jnp.where(core == 0, hidden[:, :, :n], hidden[:, :, keep - n :])
        mine = mine.astype(out_ref.dtype)
        for i in range(2):
            out_ref[pl.ds(i * pairs + offsets[c], GROUPS[c]), :] = mine[i]

    copy(last, me, ACROSS).start()
    for c in range(n_a):
        along(c, me, UP)
        along(c, me, DOWN)
        copy(c, me, ACROSS).start()
    along(last, me, UP)
    along(last, me, DOWN)
    copy(last, at(z, 1 - y), ACROSS).wait_recv()
    along(last, at(z, 1 - y), UP)
    along(last, at(z, 1 - y), DOWN)

    def start_sums():
        w_copy.wait()
        add(me, 0, pairs, fresh=True)

    def peer_sums():
        wait_across(z)
        add(at(z, 1 - y), 0, pairs)

    tasks = {
        (1, 0): start_sums,
        (2, 0): lambda: add_at(1, False),
        (2, 1): peer_sums,
        (3, 0): lambda: add_at(2, False),
        (3, 1): lambda: add_at(1, True),
    }
    for d in range(1, Z):
        for c in range(n_a):
            pass_on(c, d)
            if (d, c) in tasks:
                tasks[d, c]()
        if d < Z - 1:
            pass_on(last, d)

    add_at(2, True)
    add(at(far, y), 0, offsets[last])
    def far_piece(c):
        copy(c, at(far, 1 - y), ACROSS).wait_recv()
        add(at(far, 1 - y), offsets[c], GROUPS[c])
        swap(c).start()

    for c in range(n_a - 1):
        far_piece(c)
        if c > 0:
            finish(c - 1)
    pass_on(last, Z - 1)
    for yy in range(Y):
        add(at(far, yy), offsets[last], GROUPS[last])
    swap(last).start()
    finish(n_a - 2)
    finish(last)
    far_piece(n_a - 1)
    finish(n_a - 1)

    copy(last, me, ACROSS).wait_send()
    for c in range(len(GROUPS)):
        swap(c).wait_send()
        for zs in range(Z):
            if c != last:
                copy(c, at(zs, y), ACROSS).wait_send()
            for way, sent in ((UP, (zs <= z) & (z < Z - 1)), (DOWN, (zs >= z) & (z > 0))):
                @pl.when(sent)
                def _():
                    for yy in range(Y) if c == last else (y,):
                        copy(c, at(zs, yy), way).wait_send()


def fused(n_wide, activations, up_weight):
    rows, cols = activations.shape
    depth, units = up_weight.shape
    keep = (units // 2 + LANES - 1) // LANES * LANES
    return pl.pallas_call(
        functools.partial(kernel, n_wide),
        out_shape=jax.ShapeDtypeStruct((rows, units // 2), jnp.bfloat16),
        in_specs=[
            pl.BlockSpec(memory_space=pltpu.VMEM),
            pl.BlockSpec(memory_space=pl.ANY),
        ],
        out_specs=pl.BlockSpec(memory_space=pltpu.VMEM),
        scratch_shapes=[
            pltpu.VMEM((n_wide, rows // 2, 2 * cols), jnp.bfloat16),
            pltpu.VMEM((depth, units), jnp.bfloat16),
            pltpu.VMEM((2, rows // 2, units), jnp.float32),
            pltpu.VMEM((2, rows // 2, keep), jnp.float32),
            pltpu.SemaphoreType.DMA,
            pltpu.SemaphoreType.DMA((len(GROUPS), 3, n_wide)),
            pltpu.SemaphoreType.DMA((len(GROUPS), n_wide)),
            pltpu.SemaphoreType.DMA((len(GROUPS),)),
            pltpu.SemaphoreType.DMA((len(GROUPS),)),
        ],
        compiler_params=pltpu.CompilerParams(
            collective_id=0, has_side_effects=True, vmem_limit_bytes=48 * 2**20
        ),
        cost_estimate=pl.CostEstimate(
            flops=2 * rows * depth * units,
            bytes_accessed=2 * depth * units,
            transcendentals=rows * units // 2,
        ),
    )(activations.T, up_weight)


def solution(mesh):
    n_wide = mesh.shape["wide"]
    body = functools.partial(fused, n_wide) if n_wide == 4 * Y else plain
    return jax.shard_map(
        body,
        mesh=mesh,
        in_specs=(P("groups", ("narrow", "wide")), P("narrow", "wide")),
        out_specs=P("groups", ("wide", "narrow")),
        check_vma=False,
    )
```
